32 devices in a mesh: plane: 2 (over x), slab: 16 (over z, y, core).
Axes of the slice: x: 2, y: 2, z: 4, core: 2. Of those that a mesh axis runs over, the one named last changes fastest.
Arguments:
- kappa: float32 [2, 4096, 4096], P('plane', 'slab'), may hold values from -2.5 to 2.5
- ray_offsets: float32 [2, 16, 2, 32, 4096], P(None, 'slab', 'plane'), may hold values from -0.5 to 0.5
Outputs:
- deflection: float32 [2, 16, 2, 32, 4096], P(None, 'slab', 'plane')
- jacobian: float32 [4, 16, 2, 32, 4096], P(None, 'slab', 'plane')
The draws below stay inside these ranges and needn't reach their ends.
All inputs are finite; a program needn't handle non-finite values.
Results may differ from the reference program's by a relative error of at most 0.0003.
Values sent between devices are 32-bit elements; how exact they have to be, the bound alone decides.
A program may use at most 128 MiB of HBM per device.

```python
import jax
import jax.numpy as jnp
from jax import lax

N = 4096
PLANES = 2
SLABS = 16
STEP = 4
RAYROWS = 32
MARGIN = 8
PATCH_ROWS = 16
BLOCK = 64


def draw_kappa(key, part):
    shape = (PLANES, N, N)
    return jnp.clip(0.5 * jax.random.normal(key, shape, jnp.float32), -2.5, 2.5)


def block_scale(key, extent, cuts, least, largest):
    loudness = 1.0
    for dim, parts in cuts:
        heights = jax.random.uniform(jax.random.fold_in(jax.random.fold_in(key, 6), dim), (parts,), jnp.float32, least / len(cuts), largest / len(cuts))
        loudness = loudness * jnp.repeat(jnp.exp(heights), extent[dim] // parts).reshape((-1,) + (1,) * (len(extent) - 1 - dim))
    return loudness


def setup_inputs(seed: int = 0) -> dict:
    arg_keys = jax.random.split(jax.random.key(seed), 3)
    return {
        "kappa": draw_kappa(jax.random.fold_in(arg_keys[2], 71), 0),
        "ray_offsets": jnp.clip(jax.random.uniform(arg_keys[1], (2, SLABS, PLANES, RAYROWS, N), jnp.float32, -0.5, 0.5) * block_scale(arg_keys[1], (2, SLABS, PLANES, RAYROWS, N), ((1, 16), (2, 2)), -0.4, 0.0), -0.5, 0.5),
    }


lens_ratio = 0.5
screen_modes = 4.0


def solve_plane(plane):
    length = plane.shape[0]
    indices = jnp.arange(length)
    folded = jnp.minimum(indices, length - indices).astype(plane.dtype)
    wave = (2.0 * jnp.pi / length) * folded
    screen = (2.0 * jnp.pi * screen_modes / length) ** 2
    denom = wave[:, None] ** 2 + wave[None, :] ** 2 + screen
    anchor = (indices[:, None] == 0) & (indices[None, :] == 0)
    factor = jnp.where(anchor, 0.0, -2.0 / denom).astype(plane.dtype)
    return jnp.real(jnp.fft.ifft2(jnp.fft.fft2(plane) * factor)).astype(plane.dtype)


def spline_terms(offset):
    magnitude = jnp.abs(offset)
    inside = magnitude < 1.0
    remain = jnp.maximum(2.0 - magnitude, 0.0)
    weights = jnp.where(inside, 2.0 / 3.0 - magnitude * magnitude + 0.5 * magnitude * magnitude * magnitude, remain * remain * remain / 6.0)
    slopes = jnp.sign(offset) * jnp.where(inside, -2.0 * magnitude + 1.5 * magnitude * magnitude, -0.5 * remain * remain)
    curves = jnp.where(inside, 3.0 * magnitude - 2.0, remain)
    return weights, slopes, curves


def lens_fields(plane_blocks, ycoord, xcoord):
    column_ids = jnp.arange(plane_blocks.shape[2]).astype(xcoord.dtype)
    row_ids = jnp.arange(plane_blocks.shape[0]).astype(ycoord.dtype)
    x_weights = jnp.stack(spline_terms(xcoord[:, :, None] - column_ids), axis=1)
    across = jnp.einsum("pbc,bkrc->bkpr", plane_blocks, x_weights, precision=lax.Precision.HIGHEST)
    down_weights, down_slopes, down_curves = spline_terms(ycoord[:, None, :] - row_ids[:, None])
    slope_down = jnp.sum(down_slopes * across[:, 0], axis=1)
    slope_across = jnp.sum(down_weights * across[:, 1], axis=1)
    bend_down = jnp.sum(down_curves * across[:, 0], axis=1)
    bend_across = jnp.sum(down_weights * across[:, 2], axis=1)
    bend_mixed = jnp.sum(down_slopes * across[:, 1], axis=1)
    return slope_down, slope_across, bend_down, bend_across, bend_mixed


def ray_row_outputs(window, shift_y, shift_x):
    grid_width = shift_y.shape[0]
    block_count = grid_width // BLOCK
    column_view = window.reshape(window.shape[0], PATCH_ROWS, block_count + 1, BLOCK)
    blocks = jnp.concatenate([column_view[:, :, :-1], column_view[:, :, 1:]], axis=3)
    centre_row = PATCH_ROWS // 2 - 1
    ycoord = centre_row + STEP * shift_y.reshape(block_count, BLOCK)
    xcoord = BLOCK // 2 + jnp.arange(BLOCK).astype(shift_x.dtype) + shift_x.reshape(block_count, BLOCK)
    first = lens_fields(blocks[0], ycoord, xcoord)
    second = lens_fields(blocks[1], ycoord - lens_ratio * first[0], xcoord - lens_ratio * first[1])
    hess_yy, hess_xx, hess_xy = first[2], first[3], first[4]
    other_yy, other_xx, other_xy = second[2], second[3], second[4]
    lensed_yy = 1.0 - lens_ratio * hess_yy
    lensed_xx = 1.0 - lens_ratio * hess_xx
    lensed_xy = -lens_ratio * hess_xy
    entry_yy = 1.0 - hess_yy - (other_yy * lensed_yy + other_xy * lensed_xy)
    entry_yx = -hess_xy - (other_yy * lensed_xy + other_xy * lensed_xx)
    entry_xy = -hess_xy - (other_xy * lensed_yy + other_xx * lensed_xy)
    entry_xx = 1.0 - hess_xx - (other_xy * lensed_xy + other_xx * lensed_xx)
    deflect = jnp.stack([first[0] + second[0], first[1] + second[1]]).reshape(2, grid_width)
    jacob = jnp.stack([entry_yy, entry_yx, entry_xy, entry_xx]).reshape(4, grid_width)
    return deflect, jacob


def reference(kappa, ray_offsets):
    potentials = jnp.stack([solve_plane(kappa[0]), solve_plane(kappa[1])])
    padded = jnp.pad(potentials, ((0, 0), (MARGIN, MARGIN), (BLOCK // 2, BLOCK // 2)), mode="wrap")
    ray_total = SLABS * PLANES * RAYROWS
    offsets = ray_offsets.reshape(2, ray_total, N)
    centre_row = PATCH_ROWS // 2 - 1

    def one_row(packed):
        ray_row, shift_y, shift_x = packed
        first_row = (STEP * ray_row + (STEP // 2 - centre_row + MARGIN)).astype(jnp.int32)
        window = lax.dynamic_slice_in_dim(padded, first_row, PATCH_ROWS, 1)
        return ray_row_outputs(window, shift_y, shift_x)

    deflect, jacob = lax.map(one_row, (jnp.arange(ray_total, dtype=jnp.int32), offsets[0], offsets[1]))
    deflection = jnp.transpose(deflect, (1, 0, 2)).reshape(2, SLABS, PLANES, RAYROWS, N)
    jacobian = jnp.transpose(jacob, (1, 0, 2)).reshape(4, SLABS, PLANES, RAYROWS, N)
    return deflection, jacobian
```

```python
import functools
import math

import jax
import jax.numpy as jnp
import ml_dtypes
import numpy as np
from jax import lax
from jax.experimental import pallas as pl
from jax.experimental.pallas import tpu as pltpu
from jax.sharding import PartitionSpec as P

STEP = 4
MARGIN = 8
PATCH_ROWS = 16
BLOCK = 64
RADIX = 16
LANES = 128
GROUP = 8

lens_ratio = 0.5
screen_modes = 4.0


def pair_residues():
    return [(0, RADIX // 2)] + [(r, RADIX - r) for r in range(1, RADIX // 2)]


def pair_tables(length):
    inner = length // RADIX
    n = np.arange(inner)[:, None]
    q = np.arange(inner)[None, :]
    tables = np.zeros((RADIX // 2, 2 * inner, 2 * inner))

    def angle(residue):
        return 2.0 * np.pi * (((RADIX * q + residue) * n) % length) / length

    for p, (first, second) in enumerate(pair_residues()):
        a, b = angle(first), angle(second)
        tables[p, :inner, :inner] = np.cos(a) + np.sin(a)
        if p == 0:
            tables[p, inner:, inner:] = np.cos(b) + np.sin(b)
        else:
            tables[p, inner:, :inner] = np.cos(a) - np.sin(a)
            tables[p, :inner, inner:] = np.cos(b) + np.sin(b)
            tables[p, inner:, inner:] = -(np.cos(b) - np.sin(b))
    return tables


def split_table(table, count):
    parts = []
    for _ in range(count):
        parts.append(table.astype(ml_dtypes.bfloat16))
        table = table - parts[-1].astype(np.float64)
    return np.stack(parts, axis=1)


def split(values, count):
    parts = []
    for _ in range(count):
        parts.append(values.astype(jnp.bfloat16))
        values = values - parts[-1].astype(jnp.float32)
    return parts


def split_dot(left, right, right_axis=0):
    total = None
    for order in range(len(left) - 1, -1, -1):
        for i in range(order + 1):
            term = lax.dot_general(
                left[i],
                right[order - i],
                (((1,), (right_axis,)), ((), ())),
                preferred_element_type=jnp.float32,
            )
            total = term if total is None else total + term
    return total


def weighted(terms):
    total = None
    for value, weight in terms:
        if abs(weight) < 1e-12:
            continue
        if abs(weight - 1.0) < 1e-12:
            total = value if total is None else total + value
        elif abs(weight + 1.0) < 1e-12:
            total = -value if total is None else total - value
        else:
            total = weight * value if total is None else total + weight * value
    return total


def cosine_sums(e):
    half = RADIX // 2
    quarter = half // 2
    fold = [e[i] + e[half - i] for i in range(quarter)] + [e[quarter]]
    diff = [e[i] - e[half - i] for i in range(quarter)]
    return [
        weighted(
            (v, math.cos(2.0 * math.pi * i * r / RADIX))
            for i, v in enumerate(fold if r % 2 == 0 else diff)
        )
        for r in range(half + 1)
    ]


def sine_sums(o):
    half = RADIX // 2
    quarter = half // 2
    odd = [None] + [o[i] + o[half - i] for i in range(1, quarter)] + [o[quarter]]
    even = [None] + [o[i] - o[half - i] for i in range(1, quarter)]
    sums = [None]
    for r in range(1, half):
        terms = odd if r % 2 == 1 else even
        sums.append(
            weighted(
                (terms[i], math.sin(2.0 * math.pi * i * r / RADIX)) for i in range(1, len(terms))
            )
        )
    return sums


def radix_forward(x):
    half = RADIX // 2
    e = [x[0]] + [x[i] + x[RADIX - i] for i in range(1, half)] + [x[half]]
    o = [None] + [x[i] - x[RADIX - i] for i in range(1, half)]
    c = cosine_sums(e)
    s = sine_sums(o)
    return [(c[0], c[half])] + [(c[r], s[r]) for r in range(1, half)]


def radix_inverse(pairs):
    half = RADIX // 2
    even = cosine_sums([pairs[0][0]] + [pairs[r][0] for r in range(1, half)] + [pairs[0][1]])
    odd = sine_sums([None] + [pairs[r][1] for r in range(1, half)])
    out = [None] * RADIX
    out[0], out[half] = even[0], even[half]
    for i in range(1, half):
        out[i] = even[i] + odd[i]
        out[RADIX - i] = even[i] - odd[i]
    return out


def lane_slices(width):
    size = min(width, LANES)
    return [(start, size) for start in range(0, width, size)]


def rows_forward_kernel(x_ref, table_ref, out_ref, high, low):
    rows, length = x_ref.shape
    inner = length // RADIX
    piece = out_ref.shape[2]

    @pl.when(pl.program_id(0) == 0)
    def _():
        def body(i, carry):
            here = pl.ds(pl.multiple_of(i * 16, 16), 16)
            for start, size in lane_slices(inner):
                chunks = [
                    x_ref[here, l * inner + start : l * inner + start + size] for l in range(RADIX)
                ]
                for p, pair in enumerate(radix_forward(chunks)):
                    for part, values in enumerate(pair):
                        h, w = split(values, 2)
                        at = slice(part * inner + start, part * inner + start + size)
                        high[p, here, at] = h
                        low[p, here, at] = w
            return carry

        lax.fori_loop(0, rows // 16, body, 0)

    p = pl.program_id(0)
    result = split_dot((high[p], low[p]), (table_ref[0, 0], table_ref[0, 1]), 1)
    for k in range(out_ref.shape[0]):
        out_ref[k] = result[:, k * piece : (k + 1) * piece]


def columns_kernel(planes, x_ref, table_ref, wave_ref, out_ref, high, low, rest, mixed, strips):
    length, width = x_ref.shape
    inner = length // RADIX
    pair_count = RADIX // 2
    step = pl.program_id(0)
    count, strip = strips.shape[0], strips.shape[1]

    @pl.when(step == 0)
    def _():
        def body(i, carry):
            for start, size in lane_slices(width):
                lanes = slice(start, start + size)
                chunks = [
                    x_ref[pl.ds(pl.multiple_of(l * inner + i * 16, 16), 16), lanes]
                    for l in range(RADIX)
                ]
                for p, pair in enumerate(radix_forward(chunks)):
                    for part, values in enumerate(pair):
                        h, w = split(values, 2)
                        here = pl.ds(pl.multiple_of(part * inner + i * 16, 16), 16)
                        high[p, here, lanes] = h
                        low[p, here, lanes] = w
            return carry

        lax.fori_loop(0, inner // 16, body, 0)

    @pl.when(step < pair_count)
    def _():
        p = step
        spectrum = split_dot((table_ref[0, 0], table_ref[0, 1]), (high[p], low[p]))
        row = lax.broadcasted_iota(jnp.int32, spectrum.shape, 0)
        second = jnp.where(p == 0, RADIX // 2, RADIX - p)
        index = jnp.where(row < inner, RADIX * row + p, RADIX * (row - inner) + second)
        folded = jnp.minimum(index, length - index).astype(jnp.float32)
        wave = (2.0 * math.pi / length) * folded
        column = wave_ref[...]
        screen = (2.0 * math.pi * screen_modes / length) ** 2
        denom = (wave * wave + column * column + screen) * float(length * length)
        factor = jnp.where((index == 0) & (column == 0.0), 0.0, -2.0 / denom)
        high[p], low[p], rest[p] = split(spectrum * factor, 3)

    @pl.when(step >= pair_count)
    def _():
        p = step - pair_count
        mixed[p] = split_dot(
            tuple(table_ref[0, k] for k in range(3)), (high[p], low[p], rest[p])
        )

    @pl.when(step == 2 * pair_count - 1)
    def _():
        per_chunk = inner // strip

        def body(i, carry):
            t = i * 16 // strip
            here = pl.ds(pl.multiple_of(i * 16 % strip, 16), 16)
            for start, size in lane_slices(width):
                lanes = slice(start, start + size)
                pairs = [
                    tuple(
                        mixed[p, pl.ds(pl.multiple_of(part * inner + i * 16, 16), 16), lanes]
                        for part in range(2)
                    )
                    for p in range(pair_count)
                ]
                for l, values in enumerate(radix_inverse(pairs)):
                    strips[l * per_chunk + t, here, lanes] = values
            return carry

        lax.fori_loop(0, inner // 16, body, 0)
        held = strip // STEP
        edge = MARGIN // STEP
        full = held + 2 * edge

        def assemble(t, carry):
            before = lax.rem(t + count - 1, count)
            after = lax.rem(t + 1, count)
            dest = lax.rem(t, planes) * (count // planes) + t // planes
            for m in range(STEP):
                base = m * full
                out_ref[dest, base : base + edge] = strips[
                    before, (m + 1) * held - edge : (m + 1) * held
                ]
                out_ref[dest, base + edge : base + edge + held] = strips[
                    t, m * held : (m + 1) * held
                ]
                out_ref[dest, base + edge + held : base + full] = strips[
                    after, m * held : m * held + edge
                ]
            return carry

        lax.fori_loop(0, count, assemble, 0)


def rows_inverse_kernel(x_ref, table_ref, out_ref, mixed):
    planes, pieces, rows, piece = x_ref.shape
    length = out_ref.shape[2]
    inner = length // RADIX
    p = pl.program_id(0)
    for plane in range(planes):
        total = None
        for k in range(pieces):
            at = slice(k * piece, (k + 1) * piece)
            term = split_dot(
                split(x_ref[plane, k], 3), tuple(table_ref[0, j, at, :] for j in range(3))
            )
            total = term if total is None else total + term
        mixed[plane, p] = total

    @pl.when(p == RADIX // 2 - 1)
    def _():
        for plane in range(planes):

            def body(i, carry):
                here = pl.ds(pl.multiple_of(i * 8, 8), 8)
                for start, size in lane_slices(inner):
                    pairs = [
                        tuple(
                            mixed[
                                plane, k, here, part * inner + start : part * inner + start + size
                            ]
                            for part in range(2)
                        )
                        for k in range(RADIX // 2)
                    ]
                    for l, values in enumerate(radix_inverse(pairs)):
                        out_ref[plane, here, l * inner + start : l * inner + start + size] = values
                return carry

            lax.fori_loop(0, rows // 8, body, 0)


def spline_terms(t):
    a = jnp.abs(t)
    p = jnp.maximum(2.0 - a, 0.0)
    q = jnp.maximum(1.0 - a, 0.0)
    p2 = p * p
    q2 = q * q
    weight = (p2 * p) * (1.0 / 6.0) - (q2 * q) * (2.0 / 3.0)
    slope = 2.0 * q2 - 0.5 * p2
    slope = jnp.where(t < 0.0, -slope, slope)
    return weight, slope, p - 4.0 * q


def rays_kernel(pot_ref, shift_ref, deflect_ref, jacob_ref, near, moved, down, first, total):
    rows, length = pot_ref.shape[1], pot_ref.shape[2]
    width = shift_ref.shape[2]
    groups = shift_ref.shape[1] // GROUP
    quota = rows // STEP
    centre = PATCH_ROWS // 2 - 1
    base_row = STEP // 2 - centre + MARGIN
    lane = lax.broadcasted_iota(jnp.int32, (rows, LANES), 1)

    def row_start(e, g):
        offset = base_row + centre + e
        return (offset % STEP) * quota + offset // STEP + GROUP * g

    def tile(s, carry):
        here = pl.ds(pl.multiple_of(s * LANES, LANES), LANES)
        origin = pl.program_id(0) * width + s * LANES

        def columns(plane, start):
            return pot_ref[plane, :, pl.ds(pl.multiple_of(start, LANES), LANES)]

        after = lax.rem(origin + LANES, length)
        before = lax.rem(origin + length - LANES, length)

        def shifted(plane, d):
            if isinstance(d, int) and d == 0:
                return columns(plane, origin)
            if isinstance(d, int):
                turn = -d % LANES
                other = after if d > 0 else before
            else:
                turn = lax.rem(2 * LANES - d, LANES)
                other = jnp.where(d >= 0, after, before)
            place = lane + d
            return jnp.where(
                (place >= 0) & (place < LANES),
                pltpu.roll(columns(plane, origin), turn, 1),
                pltpu.roll(columns(plane, other), turn, 1),
            )

        for k in range(5):
            near[k] = shifted(0, k - 2)

        bounds = None
        for g in range(groups):
            at = slice(g * GROUP, (g + 1) * GROUP)
            y = STEP * shift_ref[0, at, here]
            x = shift_ref[1, at, here]
            across = [spline_terms(x - float(k - 2)) for k in range(5)]
            sums = [None] * 5
            for e in range(-3, 4):
                r = row_start(e, g)
                cells = [near[k, r : r + GROUP, :] for k in range(5)]
                a0, a1, a2 = [
                    functools.reduce(
                        lambda u, v: u + v, [across[k][i] * cells[k] for k in range(5)]
                    )
                    for i in range(3)
                ]
                w, sl, cu = spline_terms(y - float(e))
                terms = (sl * a0, w * a1, cu * a0, w * a2, sl * a1)
                sums = [b if a is None else a + b for a, b in zip(sums, terms)]
            y2 = y - lens_ratio * sums[0]
            x2 = x - lens_ratio * sums[1]
            for k in range(5):
                first[g, k] = sums[k]
            first[g, 5] = y2
            first[g, 6] = x2
            mine = (y2, y2, x2, x2)
            if bounds is None:
                bounds = mine
            else:
                bounds = tuple(
                    jnp.minimum(a, b) if k % 2 == 0 else jnp.maximum(a, b)
                    for k, (a, b) in enumerate(zip(bounds, mine))
                )
        reach = float(2 * BLOCK)
        y_low = jnp.min(bounds[0])
        y_high = jnp.max(bounds[1])
        x_low = jnp.min(jnp.floor(jnp.clip(bounds[2], -reach, reach))).astype(jnp.int32)
        x_high = jnp.max(jnp.floor(jnp.clip(bounds[3], -reach, reach))).astype(jnp.int32)
        most = 2 * BLOCK - BLOCK // 2 - 1
        d_low = jnp.maximum(x_low - 1, -most)
        d_high = jnp.minimum(x_high + 2, most)

        def second(taps):
            for g in range(groups):
                y2 = first[g, 5]
                for e in taps:
                    w, sl, cu = spline_terms(y2 - float(e))
                    down[g, e + centre, 0] = w
                    down[g, e + centre, 1] = sl
                    down[g, e + centre, 2] = cu

            def column(d, c):
                cell = lax.rem(lane, BLOCK) + (BLOCK // 2) + d
                inside = (cell >= 0) & (cell < 2 * BLOCK)
                moved[...] = jnp.where(inside, shifted(1, d), 0.0)
                for g in range(groups):
                    b0 = b1 = b2 = None
                    for e in taps:
                        r = row_start(e, g)
                        cells = moved[r : r + GROUP, :]
                        t0 = down[g, e + centre, 0] * cells
                        t1 = down[g, e + centre, 1] * cells
                        t2 = down[g, e + centre, 2] * cells
                        b0 = t0 if b0 is None else b0 + t0
                        b1 = t1 if b1 is None else b1 + t1
                        b2 = t2 if b2 is None else b2 + t2
                    w, sl, cu = spline_terms(first[g, 6] - d.astype(jnp.float32))
                    terms = (w * b1, sl * b0, w * b2, cu * b0, sl * b1)
                    for k in range(5):
                        total[g, k] = total[g, k] + terms[k]
                return c

            lax.fori_loop(d_low, d_high + 1, column, 0)

        total[...] = jnp.zeros_like(total)
        narrow = (y_low >= -4.0) & (y_high <= 4.0)

        @pl.when(narrow)
        def _():
            second(range(-5, 6))

        @pl.when(jnp.logical_not(narrow))
        def _():
            second(range(-centre, PATCH_ROWS - centre))

        for g in range(groups):
            at = slice(g * GROUP, (g + 1) * GROUP)
            hess_yy, hess_xx, hess_xy = first[g, 2], first[g, 3], first[g, 4]
            other_yy, other_xx, other_xy = total[g, 2], total[g, 3], total[g, 4]
            lensed_yy = 1.0 - lens_ratio * hess_yy
            lensed_xx = 1.0 - lens_ratio * hess_xx
            lensed_xy = -lens_ratio * hess_xy
            deflect_ref[0, at, here] = first[g, 0] + total[g, 0]
            deflect_ref[1, at, here] = first[g, 1] + total[g, 1]
            jacob_ref[0, at, here] = (
                1.0 - hess_yy - (other_yy * lensed_yy + other_xy * lensed_xy)
            )
            jacob_ref[1, at, here] = -hess_xy - (other_yy * lensed_xy + other_xy * lensed_xx)
            jacob_ref[2, at, here] = -hess_xy - (other_xy * lensed_yy + other_xx * lensed_xy)
            jacob_ref[3, at, here] = (
                1.0 - hess_xx - (other_xy * lensed_xy + other_xx * lensed_xx)
            )
        return carry

    lax.fori_loop(0, width // LANES, tile, 0)


def params():
    return pltpu.CompilerParams(
        dimension_semantics=("arbitrary",), vmem_limit_bytes=56 * 1024 * 1024
    )


def on_device(tables, kappa, ray_offsets):
    rows, length = kappa.shape[1], kappa.shape[2]
    slabs = lax.axis_size("slab")
    planes = lax.axis_size("plane")
    strip = rows // planes
    padded = strip + 2 * MARGIN
    piece = length // slabs
    inner = length // RADIX
    pairs = RADIX // 2
    per_pair = 2 * inner // piece
    f32, bf16 = jnp.float32, jnp.bfloat16
    row_block = (1, 2, 2 * inner, 2 * inner)
    table_block = (1, 3, 2 * inner, 2 * inner)

    forward = pl.pallas_call(
        rows_forward_kernel,
        grid=(pairs,),
        in_specs=[
            pl.BlockSpec((rows, length), lambda i: (0, 0)),
            pl.BlockSpec(row_block, lambda i: (i, 0, 0, 0)),
        ],
        out_specs=pl.BlockSpec((per_pair, rows, piece), lambda i: (i, 0, 0)),
        out_shape=jax.ShapeDtypeStruct((slabs, rows, piece), f32),
        scratch_shapes=[pltpu.VMEM((pairs, rows, 2 * inner), bf16)] * 2,
        compiler_params=params(),
        name="rows_forward",
    )(kappa[0], tables)

    gathered = lax.all_to_all(forward, "slab", split_axis=0, concat_axis=0, tiled=True)

    position = lax.axis_index("slab") * piece + jnp.arange(piece, dtype=jnp.int32)
    pair = position // (2 * inner)
    half = position // inner % 2
    other = jnp.where(pair == 0, RADIX // 2, RADIX - pair)
    index = RADIX * (position % inner) + jnp.where(half == 0, pair, other)
    folded = jnp.minimum(index, length - index).astype(f32)
    wave = ((2.0 * math.pi / length) * folded)[None, :]

    strips = pl.pallas_call(
        functools.partial(columns_kernel, planes),
        grid=(2 * pairs,),
        in_specs=[
            pl.BlockSpec((length, piece), lambda i: (0, 0)),
            pl.BlockSpec(table_block, lambda i: (i, 0, 0, 0)),
            pl.BlockSpec((1, piece), lambda i: (0, 0)),
        ],
        out_specs=pl.BlockSpec((planes * slabs, padded, piece), lambda i: (0, 0, 0)),
        out_shape=jax.ShapeDtypeStruct((planes * slabs, padded, piece), f32),
        scratch_shapes=[
            pltpu.VMEM((pairs, 2 * inner, piece), bf16),
            pltpu.VMEM((pairs, 2 * inner, piece), bf16),
            pltpu.VMEM((pairs, 2 * inner, piece), bf16),
            pltpu.VMEM((pairs, 2 * inner, piece), f32),
            pltpu.VMEM((planes * slabs, strip, piece), f32),
        ],
        compiler_params=params(),
        name="columns",
    )(gathered.reshape(length, piece), tables, wave)

    arrived = lax.all_to_all(strips, ("plane", "slab"), split_axis=0, concat_axis=0, tiled=True)

    potential = pl.pallas_call(
        rows_inverse_kernel,
        grid=(pairs,),
        in_specs=[
            pl.BlockSpec((planes, per_pair, padded, piece), lambda i: (0, i, 0, 0)),
            pl.BlockSpec(table_block, lambda i: (i, 0, 0, 0)),
        ],
        out_specs=pl.BlockSpec((planes, padded, length), lambda i: (0, 0, 0)),
        out_shape=jax.ShapeDtypeStruct((planes, padded, length), f32),
        scratch_shapes=[pltpu.VMEM((planes, pairs, padded, 2 * inner), f32)],
        compiler_params=params(),
        name="rows_inverse",
    )(arrived.reshape(planes, slabs, padded, piece), tables)

    ray_rows = ray_offsets.shape[3]
    groups = ray_rows // GROUP
    width = min(4 * LANES, length)
    deflect, jacob = pl.pallas_call(
        rays_kernel,
        grid=(length // width,),
        in_specs=[
            pl.BlockSpec((planes, padded, length), lambda i: (0, 0, 0)),
            pl.BlockSpec((2, ray_rows, width), lambda i: (0, 0, i)),
        ],
        out_specs=[
            pl.BlockSpec((2, ray_rows, width), lambda i: (0, 0, i)),
            pl.BlockSpec((4, ray_rows, width), lambda i: (0, 0, i)),
        ],
        out_shape=[
            jax.ShapeDtypeStruct((2, ray_rows, length), f32),
            jax.ShapeDtypeStruct((4, ray_rows, length), f32),
        ],
        scratch_shapes=[
            pltpu.VMEM((5, padded, LANES), f32),
            pltpu.VMEM((padded, LANES), f32),
            pltpu.VMEM((groups, PATCH_ROWS, 3, GROUP, LANES), f32),
            pltpu.VMEM((groups, 7, GROUP, LANES), f32),
            pltpu.VMEM((groups, 5, GROUP, LANES), f32),
        ],
        compiler_params=params(),
        name="rays",
    )(potential, ray_offsets.reshape(2, ray_rows, length))
    return (deflect[:, None, None], jacob[:, None, None])


def solution(mesh):
    placed = (P("plane", "slab", None), P(None, "slab", "plane", None, None))

    def run(kappa, ray_offsets):
        length = kappa.shape[2]
        inner = length // RADIX
        strip = kappa.shape[1] // mesh.shape["slab"] // mesh.shape["plane"]
        tables = pair_tables(length)
        order = np.arange(inner).reshape(inner // strip, strip // STEP, STEP)
        order = order.transpose(0, 2, 1).reshape(-1)
        order = np.concatenate([order, order + inner])
        tables = split_table(
            np.concatenate([tables.transpose(0, 2, 1), tables[:, order, :]], axis=0), 3
        )
        body = functools.partial(on_device, jnp.asarray(tables))
        return jax.shard_map(
            body,
            mesh=mesh,
            in_specs=placed,
            out_specs=(P(None, "slab", "plane", None, None),) * 2,
            check_vma=False,
        )(kappa, ray_offsets)

    return run
```
